32 devices in a mesh: dp: 8 (over z, x), expert: 4 (over y, core).
Axes of the slice: x: 2, y: 2, z: 4, core: 2. Of those that a mesh axis runs over, the one named last changes fastest.
Arguments:
- tokens: bfloat16 [2048, 4096], P('dp', 'expert'), may hold values from -6 to 6
- route_ids: int32 [2048, 8], P('dp'), may hold values from 0 to 31, all different within a row; in each aligned block of 256 rows (0 to 255, 256 to 511, ...) at most 128 rows name the same one
- route_gates: float32 [2048, 8], P('dp'), may hold values from 0.05 to 1
- gate_weight: bfloat16 [4, 6144, 4096], P('expert', 'dp'), may hold values from -0.09375 to 0.09375
- up_weight: bfloat16 [4, 6144, 4096], P('expert', 'dp'), may hold values from -0.09375 to 0.09375
- down_weight: bfloat16 [4, 6144, 4096], P('expert', 'dp'), may hold values from -0.21875 to 0.21875
Outputs:
- mixed: bfloat16 [2048, 4096], P('dp', 'expert')
The draws below stay inside these ranges and needn't reach their ends.
Inputs may be any that keep to these rules, and one draw needn't show every extreme that they name: `route_ids`: each row names 8 different experts; within each aligned block of 256 rows (the rows of one index of dp) no expert is named by more than 128 rows, and in some block some expert is named by exactly 128 rows.
All inputs are finite; a program needn't handle non-finite values.
Results may differ from the reference program's by a relative error of at most 0.0057.
Values may be sent and summed in bfloat16 or wider, within the bound.
A program may use at most 128 MiB of HBM per device.

```python
import math
import jax
import jax.numpy as jnp
import numpy as np
from jax import lax

D = 4096
FFW = 768
TOP = 8
EXP_DEV = 8
TOK_ROW = 256
EXPERTS = 32
TOKENS = 2048
CAP = 128
N_DP = 8


def block_levels(key, shape, cuts, low, top_value):
    loudness, own = 1.0, jax.random.fold_in(key, 6)
    for axis_at, parts in cuts:
        steps = jnp.exp(jax.random.uniform(jax.random.fold_in(own, axis_at), (parts,), jnp.float32, low / len(cuts), top_value / len(cuts)))
        loudness = loudness * jnp.repeat(steps, shape[axis_at] // parts).reshape([-1 if axis == axis_at else 1 for axis in range(len(shape))])
    return loudness


def assign_block(rng, own, number, rows, amount, top, reach, slope):
    order = jax.random.permutation(rng, amount)
    heavy_load, usual = load_shares(amount, rows * top, reach, slope, True), load_shares(amount, rows * top, reach, slope, False)
    places = jnp.arange(amount)

    def named(sizes, rotation):
        used = int((sizes > 0).sum())
        fixed = max(1, used // 4)
        moved = fixed + (places - fixed + rotation * (used - fixed)) % max(1, amount - fixed)
        return jnp.zeros((amount,), jnp.int32).at[order[jnp.where(places < fixed, places, moved)]].set(jnp.asarray(sizes, jnp.int32))

    sizes = jnp.where(number % 4 == 0, named(heavy_load, number // 4), named(usual, number - number // 4 - 1))
    mixed = jax.random.permutation(jax.random.fold_in(own, 3), amount)
    donor, sink = mixed[0:amount // 2 * 2:2], mixed[1:amount // 2 * 2:2]
    margin = jnp.minimum(sizes[donor] - 1, reach - sizes[sink]) // 2
    margin = jnp.where((donor == order[0]) | (sink == order[0]) | (sizes[sink] == 0), 0, jnp.maximum(margin, 0))
    moved = jax.random.randint(jax.random.fold_in(own, 4), (amount // 2,), 0, 1 << 20) % (margin + 1)
    sizes = sizes.at[donor].add(-moved).at[sink].add(moved)
    labels = jnp.searchsorted(jnp.cumsum(sizes), jnp.arange(rows * top), side="right").astype(jnp.int32)
    grid = labels.reshape(top, rows).T
    grid = grid[jax.random.permutation(jax.random.fold_in(own, 1), rows)]
    rotation = jax.random.randint(jax.random.fold_in(own, 2), (rows, 1), 0, top)
    return jnp.take_along_axis(grid, (jnp.arange(top)[None, :] + rotation) % top, axis=1)


def load_shares(count, total, limit, skew, full):
    portions = [(1 << 20) // math.isqrt(standing ** skew) + 1 for standing in range(1, count + 1)]
    largest = limit if full else min(limit, max(-(-total // count), total * portions[0] // sum(portions)))
    least = 1 if total - largest >= count - 1 else 0
    holding, surplus = [largest] + [least] * (count - 1), total - largest - least * (count - 1)
    while surplus > 0:
        free = [i for i in range(1, count) if holding[i] < largest] or [i for i in range(1, count) if holding[i] < limit]
        whole, budget = sum([portions[i] for i in free]), surplus
        for i in free:
            addition = min(limit - holding[i], max(1, budget * portions[i] // whole), surplus)
            holding[i] = holding[i] + addition
            surplus = surplus - addition
    return np.array(holding)


def normal_values(rng, extent, spread, bound, shards=(), kind=jnp.bfloat16):
    entries = jax.random.normal(rng, extent, jnp.float32) * spread
    if len(shards) > 0:
        entries = block_levels(rng, extent, shards, -0.22, 0.18) * entries
    return jnp.clip(entries, min=-bound, max=bound).astype(kind)


def setup_inputs(seed: int = 0) -> dict:
    seeds = jax.random.split(jax.random.key(seed), 7)
    tokens = normal_values(seeds[0], (TOKENS, D), 1.0, 6.0, ((0, 8), (1, 4)))
    route_ids_keys = jax.random.split(jax.random.fold_in(seeds[1], 1), TOKENS // TOK_ROW)
    route_ids_turns = jax.random.permutation(jax.random.fold_in(seeds[1], 3), TOKENS // TOK_ROW)
    route_ids = jax.vmap(lambda own, number: assign_block(jax.random.fold_in(seeds[1], 2), own, number, TOK_ROW, EXPERTS, TOP, CAP, 2))(route_ids_keys, route_ids_turns).reshape((TOKENS, TOP))
    route_gates = jnp.clip(jnp.exp(math.log(1.0) - 2.9957323 * jax.random.uniform(seeds[2], (TOKENS, TOP), jnp.float32) ** block_levels(seeds[2], (TOKENS, TOP), ((0, 8),), -0.2, 0.2)), 0.05, 1.0)
    gate_weight = normal_values(seeds[3], (EXPERTS // EXP_DEV, EXP_DEV * FFW, D), D ** -0.5, 0.09375, ((0, 4), (1, 8)))
    up_weight = normal_values(seeds[4], (EXPERTS // EXP_DEV, EXP_DEV * FFW, D), D ** -0.5, 0.09375, ((0, 4), (1, 8)))
    down_weight = normal_values(seeds[5], (EXPERTS // EXP_DEV, EXP_DEV * FFW, D), FFW ** -0.5, 0.21875, ((0, 4), (1, 8)))
    return dict(tokens=tokens, route_ids=route_ids, route_gates=route_gates, gate_weight=gate_weight, up_weight=up_weight, down_weight=down_weight)


def reference(tokens, route_ids, route_gates, gate_weight, up_weight, down_weight):
    gate_weight = gate_weight.reshape(EXPERTS * FFW, D)
    up_weight = up_weight.reshape(EXPERTS * FFW, D)
    down_weight = down_weight.reshape(EXPERTS * FFW, D)
    per_row = TOK_ROW * TOP
    block_ids = route_ids.reshape(N_DP, per_row).astype(jnp.int32)
    onehot = (block_ids[:, :, None] == jnp.arange(EXPERTS, dtype=jnp.int32)[None, None, :]).astype(jnp.int32)
    running = jnp.cumsum(onehot, axis=1) - 1
    position = jnp.take_along_axis(running, block_ids[:, :, None], axis=2)[:, :, 0].astype(jnp.int32)
    block_num = jnp.arange(N_DP, dtype=jnp.int32)[:, None]
    route_num = jnp.arange(per_row, dtype=jnp.int32)[None, :]
    slot = (block_ids * (N_DP * CAP) + block_num * CAP + position).astype(jnp.int32)
    owner = (block_num * TOK_ROW + route_num // TOP).astype(jnp.int32)
    owner = jnp.broadcast_to(owner, slot.shape)
    slot_token = jnp.full((EXPERTS * N_DP * CAP,), TOKENS, jnp.int32).at[slot.reshape(-1)].set(owner.reshape(-1))
    slot_gate = jnp.zeros((EXPERTS * N_DP * CAP,), jnp.float32).at[slot.reshape(-1)].set(route_gates.reshape(-1))
    slot_token = slot_token.reshape(EXPERTS, N_DP * CAP)
    slot_gate = slot_gate.reshape(EXPERTS, N_DP * CAP)
    padded = jnp.concatenate([tokens, jnp.zeros((1, D), tokens.dtype)], axis=0)
    dims = (((1,), (1,)), ((), ()))

    def one_expert(total, items):
        expert, rows_idx, gains = items
        start = (expert * FFW).astype(jnp.int32)
        gate_rows = lax.dynamic_slice_in_dim(gate_weight, start, FFW, 0)
        up_rows = lax.dynamic_slice_in_dim(up_weight, start, FFW, 0)
        down_rows = lax.dynamic_slice_in_dim(down_weight, start, FFW, 0)
        rows = padded[rows_idx]
        gate = lax.dot_general(rows, gate_rows, dims, preferred_element_type=jnp.float32)
        upper = lax.dot_general(rows, up_rows, dims, preferred_element_type=jnp.float32)
        act = (jax.nn.silu(gate) * upper).astype(jnp.bfloat16)
        result = jnp.dot(act, down_rows, preferred_element_type=jnp.float32).astype(jnp.bfloat16)
        total = total.at[rows_idx].add(gains[:, None] * result.astype(jnp.float32))
        return total, None

    start_total = jnp.zeros((TOKENS + 1, D), jnp.float32)
    experts_list = jnp.arange(EXPERTS, dtype=jnp.int32)
    total, unused = lax.scan(one_expert, start_total, (experts_list, slot_token, slot_gate))
    return total[:TOKENS].astype(jnp.bfloat16)
```

```python
import jax
import jax.numpy as jnp
from jax import lax
from jax.experimental import pallas as pl
from jax.experimental.pallas import tpu as pltpu
from jax.sharding import PartitionSpec as P

EXP_DEV = 8
MESH = pl.DeviceIdType.MESH
ORDER = (0, 1, 3, 2)
NAMES = (
    [(n, d) for n in ("z", "rz") for d in (1, 2, 3)]
    + [(n, d) for n in ("x", "y", "fx", "fy", "rx2", "ry2") for d in range(4)]
    + [(n, d, i) for n in ("p", "rx1", "ry1") for d in range(4) for i in range(2)]
    + [("s", d, i) for d in range(4) for i in range(5)]
    + [("w", m) for m in range(1, 8)]
)
SLOT = {name: i for i, name in enumerate(NAMES)}


def layer_kernel(
    tok, wt, g_hbm, u_hbm, w_hbm, out, a, gates, gw, uw, dw, sb, rx1, ry1, rx2, ry2, rz,
    act, col, send, recv, local,
):
    dp = lax.axis_index("dp")
    ex = lax.axis_index("expert")
    z, x = dp // 2, dp % 2
    y, k = ex // 2, ex % 2
    tr, tc = tok.shape
    half = tr // 2
    hid = gw.shape[0]
    x_dev = (z * 2 + (1 - x), ex)
    y_dev = (dp, (1 - y) * 2 + k)
    s_dev = (dp, y * 2 + (1 - k))

    def z_dev(d):
        return (((z + d) % 4) * 2 + x, ex)

    def row(d, xx):
        return pl.multiple_of((((z + d) % 4) * 2 + xx) * tr, tr)

    def cols(yy, kk):
        return pl.ds(pl.multiple_of((yy * 2 + kk) * tc, tc), tc)

    def blk(d, xx, yy, kk, part=None):
        if part is None:
            return a.at[pl.ds(row(d, xx), tr), cols(yy, kk)]
        start = pl.multiple_of(row(d, xx) + part * half, half)
        return a.at[pl.ds(start, half), cols(yy, kk)]

    def copy(name, src, dst, dev, there=None):
        return pltpu.make_async_remote_copy(
            src_ref=src,
            dst_ref=dst,
            send_sem=send.at[SLOT[name]],
            recv_sem=recv.at[SLOT[there or name]],
            device_id=dev,
            device_id_type=MESH,
        )

    sent = {}

    def go(name, src, dst, dev, there=None):
        c = copy(name, src, dst, dev, there)
        c.start()
        sent[name] = c

    def got(name, dst, dev):
        copy(name, dst, dst, dev).wait_recv()

    def drain(name):
        sent.pop(name).wait_send()

    barrier = pltpu.get_barrier_semaphore()
    for m in range(1, 8):
        pl.semaphore_signal(barrier, inc=1, device_id=((dp + m) % 8, ex), device_id_type=MESH)
    for dev in (y_dev, s_dev):
        pl.semaphore_signal(barrier, inc=1, device_id=dev, device_id_type=MESH)
    pl.semaphore_wait(barrier, 9)

    mine = blk(0, x, y, k)
    go(("x", 0), tok, mine, x_dev)
    go(("y", 0), tok, mine, y_dev)
    for d in (1, 3, 2):
        go(("z", d), tok, mine, z_dev(d), ("z", 4 - d))
    go(("s", 0, 0), tok, mine, s_dev)
    for m in range(1, 8):
        go(("w", m), wt, gates.at[dp], ((dp + m) % 8, ex), ("w", 8 - m))
    loads = [
        pltpu.make_async_copy(src, dst, local.at[i])
        for i, (src, dst) in enumerate(
            ((tok, mine), (wt, gates.at[dp]), (g_hbm, gw), (u_hbm, uw), (w_hbm, dw))
        )
    ]
    for load in loads:
        load.start()

    def pass_z(d):
        b = blk(d, x, y, k)
        got(("z", d), b, z_dev(d))
        go(("x", d), b, b, x_dev)
        go(("y", d), b, b, y_dev)
        go(("s", d, 0), b, b, s_dev)

    def pass_xy(d):
        b = blk(d, 1 - x, y, k)
        got(("x", d), b, x_dev)
        h = blk(d, 1 - x, y, k, 0)
        go(("fy", d), h, h, y_dev)
        go(("s", d, 1), b, b, s_dev)
        b = blk(d, x, 1 - y, k)
        got(("y", d), b, y_dev)
        h = blk(d, x, 1 - y, k, 1)
        go(("fx", d), h, h, x_dev)
        go(("s", d, 2), b, b, s_dev)

    def pass_far(d):
        h = blk(d, 1 - x, 1 - y, k, 0)
        got(("fy", d), h, y_dev)
        go(("s", d, 3), h, h, s_dev)
        h = blk(d, 1 - x, 1 - y, k, 1)
        got(("fx", d), h, x_dev)
        go(("s", d, 4), h, h, s_dev)

    def complete(d):
        got(("s", d, 0), blk(d, x, y, 1 - k), s_dev)
        got(("s", d, 1), blk(d, 1 - x, y, 1 - k), s_dev)
        got(("s", d, 2), blk(d, x, 1 - y, 1 - k), s_dev)
        got(("s", d, 3), blk(d, 1 - x, 1 - y, 1 - k, 0), s_dev)
        got(("s", d, 4), blk(d, 1 - x, 1 - y, 1 - k, 1), s_dev)

    dims = (((1,), (1,)), ((), ()))

    def hidden(d):
        rows = pl.ds(pl.multiple_of(((z + d) % 4) * 2 * tr, 2 * tr), 2 * tr)

        @pl.loop(0, hid // 256)
        def _(i):
            hs = pl.ds(pl.multiple_of(i * 256, 256), 256)
            g = lax.dot_general(a[rows, :], gw[hs, :], dims, preferred_element_type=jnp.float32)
            u = lax.dot_general(a[rows, :], uw[hs, :], dims, preferred_element_type=jnp.float32)
            act[:, hs] = ((g / (1.0 + jnp.exp(-g))) * u).astype(jnp.bfloat16)

        for xx in range(2):
            table = gates[((z + d) % 4) * 2 + xx]
            pick = lax.broadcasted_iota(jnp.int32, table.shape, 0) == dp
            line = jnp.sum(jnp.where(pick, table, 0.0), axis=0, keepdims=True)
            col[xx * tr : (xx + 1) * tr, :] = jnp.broadcast_to(line, (128, tr)).T

    def project(d):
        rows = pl.ds(pl.multiple_of(((z + d) % 4) * 2 * tr, 2 * tr), 2 * tr)
        for name in [("x", d), ("y", d), ("fx", d), ("fy", d)] + [("s", d, i) for i in range(5)]:
            drain(name)

        @pl.loop(0, a.shape[1] // 512)
        def _(i):
            cs = pl.ds(pl.multiple_of(i * 512, 512), 512)
            r = jnp.dot(act[...], dw[:, cs], preferred_element_type=jnp.float32)
            a[rows, cs] = (r * col[:, 0:1]).astype(jnp.bfloat16)

    def add(start, count, cs, extra):
        step = 64

        @pl.loop(0, count // step)
        def _(i):
            o = pl.multiple_of(i * step, step)
            rows = pl.ds(pl.multiple_of(start + o, step), step)
            a[rows, cs] = (
                a[rows, cs].astype(jnp.float32) + extra[pl.ds(o, step), :].astype(jnp.float32)
            ).astype(jnp.bfloat16)

    def reduce0(d):
        rows = pl.ds(pl.multiple_of(((z + d) % 4) * 2 * tr, 2 * tr), 2 * tr)
        for yy in range(2):
            go(("p", d, yy), a.at[rows, cols(yy, 1 - k)], sb.at[d, yy], s_dev)

    def reduce1(d):
        start = pl.multiple_of(((z + d) % 4) * 2 * tr, 2 * tr)
        for yy in range(2):
            got(("p", d, yy), sb.at[d, yy], s_dev)
            add(start, 2 * tr, cols(yy, k), sb.at[d, yy])
        for i in range(2):
            go(("ry1", d, i), blk(d, i, 1 - y, k, 0), ry1.at[d, i], y_dev)
            go(("rx1", d, i), blk(d, 1 - x, i, k, 1), rx1.at[d, i], x_dev)

    def reduce2(d):
        for i in range(2):
            got(("ry1", d, i), ry1.at[d, i], y_dev)
            add(row(d, i), half, cols(y, k), ry1.at[d, i])
        go(("rx2", d), blk(d, 1 - x, y, k, 0), rx2.at[d], x_dev)
        for i in range(2):
            got(("rx1", d, i), rx1.at[d, i], x_dev)
            add(row(d, x) + half, half, cols(i, k), rx1.at[d, i])
        go(("ry2", d), blk(d, x, 1 - y, k, 1), ry2.at[d], y_dev)

    def reduce3(d):
        got(("rx2", d), rx2.at[d], x_dev)
        add(row(d, x), half, cols(y, k), rx2.at[d])
        got(("ry2", d), ry2.at[d], y_dev)
        add(row(d, x) + half, half, cols(y, k), ry2.at[d])
        if d:
            go(("rz", d), blk(d, x, y, k), rz.at[3 - d], z_dev(d), ("rz", 4 - d))

    pass_xy(0)
    for d in (1, 3, 2):
        pass_z(d)
    loads[0].wait()
    pass_far(0)
    loads[1].wait()
    for m in range(1, 8):
        got(("w", m), gates.at[(dp + m) % 8], ((dp + m) % 8, ex))
    for load in loads[2:]:
        load.wait()

    for i, d in enumerate(ORDER):
        complete(d)
        hidden(d)
        if i < 3:
            pass_xy(ORDER[i + 1])
        project(d)
        reduce0(d)
        if i < 3:
            pass_far(ORDER[i + 1])
        if i >= 1:
            reduce1(ORDER[i - 1])
        if i >= 2:
            reduce2(ORDER[i - 2])
        if i >= 3:
            reduce3(ORDER[i - 3])
    reduce1(ORDER[3])
    reduce2(ORDER[2])
    reduce3(ORDER[1])
    reduce2(ORDER[3])
    reduce3(ORDER[2])
    reduce3(ORDER[3])
    for d in (1, 2, 3):
        got(("rz", d), rz.at[d - 1], z_dev(d))

    @pl.loop(0, tr // 64)
    def _(i):
        o = pl.multiple_of(i * 64, 64)
        total = a[pl.ds(pl.multiple_of(row(0, x) + o, 64), 64), cols(y, k)].astype(jnp.float32)
        for d in range(3):
            total = total + rz[d, pl.ds(o, 64), :].astype(jnp.float32)
        out[pl.ds(o, 64), :] = total.astype(jnp.bfloat16)

    for name in list(sent):
        drain(name)


def fused_body(tokens, route_ids, route_gates, gate_weight, up_weight, down_weight):
    tr, tc = tokens.shape
    width = gate_weight.shape[2]
    hid = gate_weight.shape[1]
    experts = lax.axis_index("expert") * EXP_DEV + jnp.arange(EXP_DEV, dtype=jnp.int32)
    hit = route_ids[None, :, :] == experts[:, None, None]
    wt = jnp.sum(jnp.where(hit, route_gates[None, :, :], 0.0), axis=2)
    half = tr // 2
    bf = jnp.bfloat16
    return pl.pallas_call(
        layer_kernel,
        out_shape=jax.ShapeDtypeStruct((tr, tc), bf),
        in_specs=[
            pl.BlockSpec(memory_space=pl.ANY),
            pl.BlockSpec(memory_space=pltpu.VMEM),
            pl.BlockSpec(memory_space=pl.ANY),
            pl.BlockSpec(memory_space=pl.ANY),
            pl.BlockSpec(memory_space=pl.ANY),
        ],
        out_specs=pl.BlockSpec(memory_space=pltpu.VMEM),
        scratch_shapes=[
            pltpu.VMEM((8 * tr, width), bf),
            pltpu.VMEM((8, EXP_DEV, tr), jnp.float32),
            pltpu.VMEM((hid, width), bf),
            pltpu.VMEM((hid, width), bf),
            pltpu.VMEM((hid, width), bf),
            pltpu.VMEM((4, 2, 2 * tr, tc), bf),
            pltpu.VMEM((4, 2, half, tc), bf),
            pltpu.VMEM((4, 2, half, tc), bf),
            pltpu.VMEM((4, half, tc), bf),
            pltpu.VMEM((4, half, tc), bf),
            pltpu.VMEM((3, tr, tc), bf),
            pltpu.VMEM((2 * tr, hid), bf),
            pltpu.VMEM((2 * tr, 128), jnp.float32),
            pltpu.SemaphoreType.DMA((len(NAMES),)),
            pltpu.SemaphoreType.DMA((len(NAMES),)),
            pltpu.SemaphoreType.DMA((5,)),
        ],
        compiler_params=pltpu.CompilerParams(
            collective_id=0, has_side_effects=True, vmem_limit_bytes=60 * 1024 * 1024
        ),
        cost_estimate=pl.CostEstimate(
            flops=6 * 8 * tr * width * hid, bytes_accessed=6 * width * hid, transcendentals=0
        ),
    )(tokens, wt, gate_weight[0], up_weight[0], down_weight[0])


def route_slots(ids_rows, first_expert, expert_count, capacity):
    tok_rows, top_k = ids_rows.shape
    flat_ids = ids_rows.reshape(-1)
    local_ids = flat_ids - first_expert
    inside = (local_ids >= 0) & (local_ids < expert_count)
    safe_ids = jnp.where(inside, local_ids, 0)
    onehot = (safe_ids[:, None] == jnp.arange(expert_count, dtype=jnp.int32)[None, :]).astype(
        jnp.int32
    )
    onehot = onehot * inside.astype(jnp.int32)[:, None]
    running = jnp.cumsum(onehot, axis=0) - 1
    position = jnp.sum(onehot * running, axis=1)
    dump_slot = expert_count * capacity
    slot_index = jnp.where(inside, safe_ids * capacity + position, dump_slot)
    owner = jnp.arange(tok_rows * top_k, dtype=jnp.int32) // top_k
    slot_token = jnp.full((dump_slot + 1,), tok_rows, jnp.int32).at[slot_index].set(owner)
    return (slot_index, slot_token[:dump_slot])


def expert_rows(rows, gate_rows, up_rows, down_rows):
    dims = (((1,), (1,)), ((), ()))
    gate = lax.dot_general(rows, gate_rows, dims, preferred_element_type=jnp.float32)
    upper = lax.dot_general(rows, up_rows, dims, preferred_element_type=jnp.float32)
    act = (jax.nn.silu(gate) * upper).astype(jnp.bfloat16)
    return jnp.dot(act, down_rows, preferred_element_type=jnp.float32)


def body(tokens, route_ids, route_gates, gate_weight, up_weight, down_weight):
    gate_local = gate_weight[0]
    up_local = up_weight[0]
    down_local = down_weight[0]
    columns = lax.axis_size("expert")
    dp_count = lax.axis_size("dp")
    blocks = dp_count // EXP_DEV
    column = lax.axis_index("expert")
    rows_all = lax.all_gather(tokens, "expert", axis=1, tiled=True)
    tok_rows, top_k = route_ids.shape
    width = rows_all.shape[1]
    capacity = 2 * tok_rows * top_k // (EXP_DEV * columns)
    slot_index, slot_token = route_slots(route_ids, column * EXP_DEV, EXP_DEV, capacity)
    padded = jnp.concatenate([rows_all, jnp.zeros((1, width), jnp.bfloat16)], axis=0)
    buffer = padded[slot_token].reshape(EXP_DEV, capacity, width)
    copies = jnp.broadcast_to(buffer[:, None], (EXP_DEV, blocks, capacity, width))
    copies = copies.reshape(dp_count, capacity, width)
    received = lax.all_to_all(copies, "dp", split_axis=0, concat_axis=0, tiled=True)
    count = received.shape[1]
    flat = received.reshape(dp_count * count, width)
    part = expert_rows(flat, gate_local, up_local, down_local)
    part = part.reshape(dp_count, count, width)
    partials = lax.all_to_all(
        part.astype(jnp.bfloat16), "dp", split_axis=0, concat_axis=0, tiled=True
    ).astype(part.dtype)
    results = jnp.sum(partials.reshape(EXP_DEV, blocks, capacity, width), axis=1).astype(
        jnp.bfloat16
    )
    results = results.reshape(EXP_DEV * capacity, width)
    results_pad = jnp.concatenate([results, jnp.zeros((1, width), jnp.bfloat16)], axis=0)
    slot_rows = slot_index.reshape(tok_rows, top_k)
    mixed = jnp.zeros((tok_rows, width), jnp.float32)
    for route in range(top_k):
        picked = results_pad[slot_rows[:, route]]
        mixed = mixed + route_gates[:, route : route + 1] * picked.astype(jnp.float32)
    summed = lax.psum_scatter(mixed, "expert", scatter_dimension=1, tiled=True)
    return summed.astype(jnp.bfloat16)


def solution(mesh):
    placed = (
        P("dp", "expert"),
        P("dp", None),
        P("dp", None),
        P("expert", "dp", None),
        P("expert", "dp", None),
        P("expert", "dp", None),
    )
    small = mesh.shape["dp"] == 8 and mesh.shape["expert"] == 4
    return jax.shard_map(
        fused_body if small else body, mesh=mesh, in_specs=placed, out_specs=P("dp", "expert"), check_vma=False
    )
```

```python
import jax
import jax.numpy as jnp
from jax import lax
from jax.experimental import pallas as pl
from jax.experimental.pallas import tpu as pltpu
from jax.sharding import PartitionSpec as P

EXP_DEV = 8
MESH = pl.DeviceIdType.MESH
ORDER = (0, 3, 2, 1)
NAMES = (
    [(n, d) for n in ("z", "rz") for d in (1, 2, 3)]
    + [(n, d) for n in ("x", "y", "fx", "fy", "rx2", "ry2") for d in range(4)]
    + [(n, d, i) for n in ("p", "rx1", "ry1") for d in range(4) for i in range(2)]
    + [("s", d, i) for d in range(4) for i in range(5)]
    + [("w", m) for m in range(1, 8)]
)
SLOT = {name: i for i, name in enumerate(NAMES)}


def layer_kernel(
    tok, wt, g_hbm, u_hbm, w_hbm, out, a, gates, gw, uw, dw, sb, rx1, ry1, rx2, ry2, rz,
    act, col, send, recv, local,
):
    dp = lax.axis_index("dp")
    ex = lax.axis_index("expert")
    z, x = dp // 2, dp % 2
    y, k = ex // 2, ex % 2
    tr, tc = tok.shape
    half = tr // 2
    hid = gw.shape[0]
    x_dev = (z * 2 + (1 - x), ex)
    y_dev = (dp, (1 - y) * 2 + k)
    s_dev = (dp, y * 2 + (1 - k))

    def z_dev(d):
        return (((z + d) % 4) * 2 + x, ex)

    def row(d, xx):
        return pl.multiple_of((((z + d) % 4) * 2 + xx) * tr, tr)

    def cols(yy, kk):
        return pl.ds(pl.multiple_of((yy * 2 + kk) * tc, tc), tc)

    def blk(d, xx, yy, kk, part=None):
        if part is None:
            return a.at[pl.ds(row(d, xx), tr), cols(yy, kk)]
        start = pl.multiple_of(row(d, xx) + part * half, half)
        return a.at[pl.ds(start, half), cols(yy, kk)]

    def copy(name, src, dst, dev, there=None):
        return pltpu.make_async_remote_copy(
            src_ref=src,
            dst_ref=dst,
            send_sem=send.at[SLOT[name]],
            recv_sem=recv.at[SLOT[there or name]],
            device_id=dev,
            device_id_type=MESH,
        )

    sent = {}

    def go(name, src, dst, dev, there=None):
        c = copy(name, src, dst, dev, there)
        c.start()
        sent[name] = c

    def got(name, dst, dev):
        copy(name, dst, dst, dev).wait_recv()

    def drain(name):
        sent.pop(name).wait_send()

    barrier = pltpu.get_barrier_semaphore()
    for m in range(1, 8):
        pl.semaphore_signal(barrier, inc=1, device_id=((dp + m) % 8, ex), device_id_type=MESH)
    for dev in (y_dev, s_dev):
        pl.semaphore_signal(barrier, inc=1, device_id=dev, device_id_type=MESH)
    pl.semaphore_wait(barrier, 9)

    mine = blk(0, x, y, k)
    go(("x", 0), tok, mine, x_dev)
    go(("y", 0), tok, mine, y_dev)
    for d in (3, 2, 1):
        go(("z", d), tok, mine, z_dev(d), ("z", 4 - d))
    go(("s", 0, 0), tok, mine, s_dev)
    for m in range(1, 8):
        go(("w", m), wt, gates.at[dp], ((dp + m) % 8, ex), ("w", 8 - m))
    loads = [
        pltpu.make_async_copy(src, dst, local.at[i])
        for i, (src, dst) in enumerate(
            ((tok, mine), (wt, gates.at[dp]), (g_hbm, gw), (u_hbm, uw), (w_hbm, dw))
        )
    ]
    for load in loads:
        load.start()

    def pass_z(d):
        b = blk(d, x, y, k)
        got(("z", d), b, z_dev(d))
        go(("x", d), b, b, x_dev)
        go(("y", d), b, b, y_dev)
        go(("s", d, 0), b, b, s_dev)

    def pass_xy(d):
        b = blk(d, 1 - x, y, k)
        got(("x", d), b, x_dev)
        h = blk(d, 1 - x, y, k, 0)
        go(("fy", d), h, h, y_dev)
        go(("s", d, 1), b, b, s_dev)
        b = blk(d, x, 1 - y, k)
        got(("y", d), b, y_dev)
        h = blk(d, x, 1 - y, k, 1)
        go(("fx", d), h, h, x_dev)
        go(("s", d, 2), b, b, s_dev)

    def pass_far(d):
        h = blk(d, 1 - x, 1 - y, k, 0)
        got(("fy", d), h, y_dev)
        go(("s", d, 3), h, h, s_dev)
        h = blk(d, 1 - x, 1 - y, k, 1)
        got(("fx", d), h, x_dev)
        go(("s", d, 4), h, h, s_dev)

    def complete(d):
        got(("s", d, 0), blk(d, x, y, 1 - k), s_dev)
        got(("s", d, 1), blk(d, 1 - x, y, 1 - k), s_dev)
        got(("s", d, 2), blk(d, x, 1 - y, 1 - k), s_dev)
        got(("s", d, 3), blk(d, 1 - x, 1 - y, 1 - k, 0), s_dev)
        got(("s", d, 4), blk(d, 1 - x, 1 - y, 1 - k, 1), s_dev)

    dims = (((1,), (1,)), ((), ()))

    def hidden(d):
        rows = pl.ds(pl.multiple_of(((z + d) % 4) * 2 * tr, 2 * tr), 2 * tr)

        @pl.loop(0, hid // 256)
        def _(i):
            hs = pl.ds(pl.multiple_of(i * 256, 256), 256)
            g = lax.dot_general(a[rows, :], gw[hs, :], dims, preferred_element_type=jnp.float32)
            u = lax.dot_general(a[rows, :], uw[hs, :], dims, preferred_element_type=jnp.float32)
            act[:, hs] = ((g / (1.0 + jnp.exp(-g))) * u).astype(jnp.bfloat16)

        for xx in range(2):
            table = gates[((z + d) % 4) * 2 + xx]
            pick = lax.broadcasted_iota(jnp.int32, table.shape, 0) == dp
            line = jnp.sum(jnp.where(pick, table, 0.0), axis=0, keepdims=True)
            col[xx * tr : (xx + 1) * tr, :] = jnp.broadcast_to(line, (128, tr)).T

    def project(d):
        rows = pl.ds(pl.multiple_of(((z + d) % 4) * 2 * tr, 2 * tr), 2 * tr)
        for name in [("x", d), ("y", d), ("fx", d), ("fy", d)] + [("s", d, i) for i in range(5)]:
            drain(name)

        @pl.loop(0, a.shape[1] // 512)
        def _(i):
            cs = pl.ds(pl.multiple_of(i * 512, 512), 512)
            r = jnp.dot(act[...], dw[:, cs], preferred_element_type=jnp.float32)
            a[rows, cs] = (r * col[:, 0:1]).astype(jnp.bfloat16)

    def add(start, count, cs, extra):
        step = 64

        @pl.loop(0, count // step)
        def _(i):
            o = pl.multiple_of(i * step, step)
            rows = pl.ds(pl.multiple_of(start + o, step), step)
            a[rows, cs] = (
                a[rows, cs].astype(jnp.float32) + extra[pl.ds(o, step), :].astype(jnp.float32)
            ).astype(jnp.bfloat16)

    def reduce0(d):
        rows = pl.ds(pl.multiple_of(((z + d) % 4) * 2 * tr, 2 * tr), 2 * tr)
        for yy in range(2):
            go(("p", d, yy), a.at[rows, cols(yy, 1 - k)], sb.at[d, yy], s_dev)

    def reduce1(d):
        start = pl.multiple_of(((z + d) % 4) * 2 * tr, 2 * tr)
        for yy in range(2):
            got(("p", d, yy), sb.at[d, yy], s_dev)
            add(start, 2 * tr, cols(yy, k), sb.at[d, yy])
        for i in range(2):
            go(("ry1", d, i), blk(d, i, 1 - y, k, 0), ry1.at[d, i], y_dev)
            go(("rx1", d, i), blk(d, 1 - x, i, k, 1), rx1.at[d, i], x_dev)

    def reduce2(d):
        for i in range(2):
            got(("ry1", d, i), ry1.at[d, i], y_dev)
            add(row(d, i), half, cols(y, k), ry1.at[d, i])
        go(("rx2", d), blk(d, 1 - x, y, k, 0), rx2.at[d], x_dev)
        for i in range(2):
            got(("rx1", d, i), rx1.at[d, i], x_dev)
            add(row(d, x) + half, half, cols(i, k), rx1.at[d, i])
        go(("ry2", d), blk(d, x, 1 - y, k, 1), ry2.at[d], y_dev)

    def reduce3(d):
        got(("rx2", d), rx2.at[d], x_dev)
        add(row(d, x), half, cols(y, k), rx2.at[d])
        got(("ry2", d), ry2.at[d], y_dev)
        add(row(d, x) + half, half, cols(y, k), ry2.at[d])
        if d:
            go(("rz", d), blk(d, x, y, k), rz.at[3 - d], z_dev(d), ("rz", 4 - d))

    pass_xy(0)
    for d in (3, 2, 1):
        pass_z(d)
    loads[0].wait()
    pass_far(0)
    loads[1].wait()
    for m in range(1, 8):
        got(("w", m), gates.at[(dp + m) % 8], ((dp + m) % 8, ex))
    for load in loads[2:]:
        load.wait()

    for i, d in enumerate(ORDER):
        complete(d)
        hidden(d)
        if i < 3:
            pass_xy(ORDER[i + 1])
        project(d)
        reduce0(d)
        if i < 3:
            pass_far(ORDER[i + 1])
        if i >= 1:
            reduce1(ORDER[i - 1])
        if i >= 2:
            reduce2(ORDER[i - 2])
        if i >= 3:
            reduce3(ORDER[i - 3])
    reduce1(ORDER[3])
    reduce2(ORDER[2])
    reduce3(ORDER[1])
    reduce2(ORDER[3])
    reduce3(ORDER[2])
    reduce3(ORDER[3])
    for d in (1, 2, 3):
        got(("rz", d), rz.at[d - 1], z_dev(d))

    @pl.loop(0, tr // 64)
    def _(i):
        o = pl.multiple_of(i * 64, 64)
        total = a[pl.ds(pl.multiple_of(row(0, x) + o, 64), 64), cols(y, k)].astype(jnp.float32)
        for d in range(3):
            total = total + rz[d, pl.ds(o, 64), :].astype(jnp.float32)
        out[pl.ds(o, 64), :] = total.astype(jnp.bfloat16)

    for name in list(sent):
        drain(name)


def fused_body(tokens, route_ids, route_gates, gate_weight, up_weight, down_weight):
    tr, tc = tokens.shape
    width = gate_weight.shape[2]
    hid = gate_weight.shape[1]
    experts = lax.axis_index("expert") * EXP_DEV + jnp.arange(EXP_DEV, dtype=jnp.int32)
    hit = route_ids[None, :, :] == experts[:, None, None]
    wt = jnp.sum(jnp.where(hit, route_gates[None, :, :], 0.0), axis=2)
    half = tr // 2
    bf = jnp.bfloat16
    return pl.pallas_call(
        layer_kernel,
        out_shape=jax.ShapeDtypeStruct((tr, tc), bf),
        in_specs=[
            pl.BlockSpec(memory_space=pl.ANY),
            pl.BlockSpec(memory_space=pltpu.VMEM),
            pl.BlockSpec(memory_space=pl.ANY),
            pl.BlockSpec(memory_space=pl.ANY),
            pl.BlockSpec(memory_space=pl.ANY),
        ],
        out_specs=pl.BlockSpec(memory_space=pltpu.VMEM),
        scratch_shapes=[
            pltpu.VMEM((8 * tr, width), bf),
            pltpu.VMEM((8, EXP_DEV, tr), jnp.float32),
            pltpu.VMEM((hid, width), bf),
            pltpu.VMEM((hid, width), bf),
            pltpu.VMEM((hid, width), bf),
            pltpu.VMEM((4, 2, 2 * tr, tc), bf),
            pltpu.VMEM((4, 2, half, tc), bf),
            pltpu.VMEM((4, 2, half, tc), bf),
            pltpu.VMEM((4, half, tc), bf),
            pltpu.VMEM((4, half, tc), bf),
            pltpu.VMEM((3, tr, tc), bf),
            pltpu.VMEM((2 * tr, hid), bf),
            pltpu.VMEM((2 * tr, 128), jnp.float32),
            pltpu.SemaphoreType.DMA((len(NAMES),)),
            pltpu.SemaphoreType.DMA((len(NAMES),)),
            pltpu.SemaphoreType.DMA((5,)),
        ],
        compiler_params=pltpu.CompilerParams(
            collective_id=0, has_side_effects=True, vmem_limit_bytes=60 * 1024 * 1024
        ),
        cost_estimate=pl.CostEstimate(
            flops=6 * 8 * tr * width * hid, bytes_accessed=6 * width * hid, transcendentals=0
        ),
    )(tokens, wt, gate_weight[0], up_weight[0], down_weight[0])


def route_slots(ids_rows, first_expert, expert_count, capacity):
    tok_rows, top_k = ids_rows.shape
    flat_ids = ids_rows.reshape(-1)
    local_ids = flat_ids - first_expert
    inside = (local_ids >= 0) & (local_ids < expert_count)
    safe_ids = jnp.where(inside, local_ids, 0)
    onehot = (safe_ids[:, None] == jnp.arange(expert_count, dtype=jnp.int32)[None, :]).astype(
        jnp.int32
    )
    onehot = onehot * inside.astype(jnp.int32)[:, None]
    running = jnp.cumsum(onehot, axis=0) - 1
    position = jnp.sum(onehot * running, axis=1)
    dump_slot = expert_count * capacity
    slot_index = jnp.where(inside, safe_ids * capacity + position, dump_slot)
    owner = jnp.arange(tok_rows * top_k, dtype=jnp.int32) // top_k
    slot_token = jnp.full((dump_slot + 1,), tok_rows, jnp.int32).at[slot_index].set(owner)
    return (slot_index, slot_token[:dump_slot])


def expert_rows(rows, gate_rows, up_rows, down_rows):
    dims = (((1,), (1,)), ((), ()))
    gate = lax.dot_general(rows, gate_rows, dims, preferred_element_type=jnp.float32)
    upper = lax.dot_general(rows, up_rows, dims, preferred_element_type=jnp.float32)
    act = (jax.nn.silu(gate) * upper).astype(jnp.bfloat16)
    return jnp.dot(act, down_rows, preferred_element_type=jnp.float32)


def body(tokens, route_ids, route_gates, gate_weight, up_weight, down_weight):
    gate_local = gate_weight[0]
    up_local = up_weight[0]
    down_local = down_weight[0]
    columns = lax.axis_size("expert")
    dp_count = lax.axis_size("dp")
    blocks = dp_count // EXP_DEV
    column = lax.axis_index("expert")
    rows_all = lax.all_gather(tokens, "expert", axis=1, tiled=True)
    tok_rows, top_k = route_ids.shape
    width = rows_all.shape[1]
    capacity = 2 * tok_rows * top_k // (EXP_DEV * columns)
    slot_index, slot_token = route_slots(route_ids, column * EXP_DEV, EXP_DEV, capacity)
    padded = jnp.concatenate([rows_all, jnp.zeros((1, width), jnp.bfloat16)], axis=0)
    buffer = padded[slot_token].reshape(EXP_DEV, capacity, width)
    copies = jnp.broadcast_to(buffer[:, None], (EXP_DEV, blocks, capacity, width))
    copies = copies.reshape(dp_count, capacity, width)
    received = lax.all_to_all(copies, "dp", split_axis=0, concat_axis=0, tiled=True)
    count = received.shape[1]
    flat = received.reshape(dp_count * count, width)
    part = expert_rows(flat, gate_local, up_local, down_local)
    part = part.reshape(dp_count, count, width)
    partials = lax.all_to_all(
        part.astype(jnp.bfloat16), "dp", split_axis=0, concat_axis=0, tiled=True
    ).astype(part.dtype)
    results = jnp.sum(partials.reshape(EXP_DEV, blocks, capacity, width), axis=1).astype(
        jnp.bfloat16
    )
    results = results.reshape(EXP_DEV * capacity, width)
    results_pad = jnp.concatenate([results, jnp.zeros((1, width), jnp.bfloat16)], axis=0)
    slot_rows = slot_index.reshape(tok_rows, top_k)
    mixed = jnp.zeros((tok_rows, width), jnp.float32)
    for route in range(top_k):
        picked = results_pad[slot_rows[:, route]]
        mixed = mixed + route_gates[:, route : route + 1] * picked.astype(jnp.float32)
    summed = lax.psum_scatter(mixed, "expert", scatter_dimension=1, tiled=True)
    return summed.astype(jnp.bfloat16)


def solution(mesh):
    placed = (
        P("dp", "expert"),
        P("dp", None),
        P("dp", None),
        P("expert", "dp", None),
        P("expert", "dp", None),
        P("expert", "dp", None),
    )
    small = mesh.shape["dp"] == 8 and mesh.shape["expert"] == 4
    return jax.shard_map(
        fused_body if small else body, mesh=mesh, in_specs=placed, out_specs=P("dp", "expert"), check_vma=False
    )
```

```python
import jax
import jax.numpy as jnp
from jax import lax
from jax.experimental import pallas as pl
from jax.experimental.pallas import tpu as pltpu
from jax.sharding import PartitionSpec as P

EXP_DEV = 8
MESH = pl.DeviceIdType.MESH
ORDER = (0, 1, 2, 3)
NAMES = (
    [(n, d) for n in ("z", "rz") for d in (1, 2, 3)]
    + [(n, d) for n in ("x", "y", "fx", "fy", "rx2", "ry2") for d in range(4)]
    + [(n, d, i) for n in ("p", "rx1", "ry1") for d in range(4) for i in range(2)]
    + [("s", d, i) for d in range(4) for i in range(5)]
    + [("w", m) for m in range(1, 8)]
)
SLOT = {name: i for i, name in enumerate(NAMES)}


def layer_kernel(
    tok, wt, g_hbm, u_hbm, w_hbm, out, a, gates, gw, uw, dw, sb, rx1, ry1, rx2, ry2, rz,
    act, col, send, recv, local,
):
    dp = lax.axis_index("dp")
    ex = lax.axis_index("expert")
    z, x = dp // 2, dp % 2
    y, k = ex // 2, ex % 2
    turn = 1 - 2 * (z // 2)
    back = 3 - 2 * (((z + 1) // 2) % 2)
    tr, tc = tok.shape
    half = tr // 2
    hid = gw.shape[0]
    x_dev = (z * 2 + (1 - x), ex)
    y_dev = (dp, (1 - y) * 2 + k)
    s_dev = (dp, y * 2 + (1 - k))

    def z_dev(d):
        return (((z + 4 + turn * d) % 4) * 2 + x, ex)

    def seen(d):
        return 2 if d == 2 else back

    def row(d, xx):
        return pl.multiple_of((((z + 4 + turn * d) % 4) * 2 + xx) * tr, tr)

    def cols(yy, kk):
        return pl.ds(pl.multiple_of((yy * 2 + kk) * tc, tc), tc)

    def blk(d, xx, yy, kk, part=None):
        if part is None:
            return a.at[pl.ds(row(d, xx), tr), cols(yy, kk)]
        start = pl.multiple_of(row(d, xx) + part * half, half)
        return a.at[pl.ds(start, half), cols(yy, kk)]

    def copy(name, src, dst, dev, there=None):
        return pltpu.make_async_remote_copy(
            src_ref=src,
            dst_ref=dst,
            send_sem=send.at[SLOT[name]],
            recv_sem=recv.at[SLOT[name] if there is None else there],
            device_id=dev,
            device_id_type=MESH,
        )

    sent = {}

    def go(name, src, dst, dev, there=None):
        c = copy(name, src, dst, dev, there)
        c.start()
        sent[name] = c

    def got(name, dst, dev):
        copy(name, dst, dst, dev).wait_recv()

    def drain(name):
        sent.pop(name).wait_send()

    barrier = pltpu.get_barrier_semaphore()
    for m in range(1, 8):
        pl.semaphore_signal(barrier, inc=1, device_id=((dp + m) % 8, ex), device_id_type=MESH)
    for dev in (y_dev, s_dev):
        pl.semaphore_signal(barrier, inc=1, device_id=dev, device_id_type=MESH)
    pl.semaphore_wait(barrier, 9)

    mine = blk(0, x, y, k)
    go(("x", 0), tok, mine, x_dev)
    go(("y", 0), tok, mine, y_dev)
    for d in (1, 2, 3):
        go(("z", d), tok, mine, z_dev(d), SLOT["z", 1] + seen(d) - 1)
    go(("s", 0, 0), tok, mine, s_dev)
    for m in range(1, 8):
        go(("w", m), wt, gates.at[dp], ((dp + m) % 8, ex), SLOT["w", 8 - m])
    loads = [
        pltpu.make_async_copy(src, dst, local.at[i])
        for i, (src, dst) in enumerate(
            ((tok, mine), (wt, gates.at[dp]), (g_hbm, gw), (u_hbm, uw), (w_hbm, dw))
        )
    ]
    for load in loads:
        load.start()

    def pass_z(d):
        b = blk(d, x, y, k)
        got(("z", d), b, z_dev(d))
        go(("x", d), b, b, x_dev)
        go(("y", d), b, b, y_dev)
        go(("s", d, 0), b, b, s_dev)

    def pass_xy(d):
        b = blk(d, 1 - x, y, k)
        got(("x", d), b, x_dev)
        h = blk(d, 1 - x, y, k, 0)
        go(("fy", d), h, h, y_dev)
        go(("s", d, 1), b, b, s_dev)
        b = blk(d, x, 1 - y, k)
        got(("y", d), b, y_dev)
        h = blk(d, x, 1 - y, k, 1)
        go(("fx", d), h, h, x_dev)
        go(("s", d, 2), b, b, s_dev)

    def pass_far(d):
        h = blk(d, 1 - x, 1 - y, k, 0)
        got(("fy", d), h, y_dev)
        go(("s", d, 3), h, h, s_dev)
        h = blk(d, 1 - x, 1 - y, k, 1)
        got(("fx", d), h, x_dev)
        go(("s", d, 4), h, h, s_dev)

    def complete(d):
        got(("s", d, 0), blk(d, x, y, 1 - k), s_dev)
        got(("s", d, 1), blk(d, 1 - x, y, 1 - k), s_dev)
        got(("s", d, 2), blk(d, x, 1 - y, 1 - k), s_dev)
        got(("s", d, 3), blk(d, 1 - x, 1 - y, 1 - k, 0), s_dev)
        got(("s", d, 4), blk(d, 1 - x, 1 - y, 1 - k, 1), s_dev)

    dims = (((1,), (1,)), ((), ()))

    def hidden(d):
        rows = pl.ds(pl.multiple_of(((z + 4 + turn * d) % 4) * 2 * tr, 2 * tr), 2 * tr)

        @pl.loop(0, hid // 256)
        def _(i):
            hs = pl.ds(pl.multiple_of(i * 256, 256), 256)
            g = lax.dot_general(a[rows, :], gw[hs, :], dims, preferred_element_type=jnp.float32)
            u = lax.dot_general(a[rows, :], uw[hs, :], dims, preferred_element_type=jnp.float32)
            act[:, hs] = ((g / (1.0 + jnp.exp(-g))) * u).astype(jnp.bfloat16)

        for xx in range(2):
            table = gates[((z + 4 + turn * d) % 4) * 2 + xx]
            pick = lax.broadcasted_iota(jnp.int32, table.shape, 0) == dp
            line = jnp.sum(jnp.where(pick, table, 0.0), axis=0, keepdims=True)
            col[xx * tr : (xx + 1) * tr, :] = jnp.broadcast_to(line, (128, tr)).T

    def project(d):
        rows = pl.ds(pl.multiple_of(((z + 4 + turn * d) % 4) * 2 * tr, 2 * tr), 2 * tr)
        for name in [("x", d), ("y", d), ("fx", d), ("fy", d)] + [("s", d, i) for i in range(5)]:
            drain(name)

        @pl.loop(0, a.shape[1] // 512)
        def _(i):
            cs = pl.ds(pl.multiple_of(i * 512, 512), 512)
            r = jnp.dot(act[...], dw[:, cs], preferred_element_type=jnp.float32)
            a[rows, cs] = (r * col[:, 0:1]).astype(jnp.bfloat16)

    def add(start, count, cs, extra):
        step = 64

        @pl.loop(0, count // step)
        def _(i):
            o = pl.multiple_of(i * step, step)
            rows = pl.ds(pl.multiple_of(start + o, step), step)
            a[rows, cs] = (
                a[rows, cs].astype(jnp.float32) + extra[pl.ds(o, step), :].astype(jnp.float32)
            ).astype(jnp.bfloat16)

    def reduce0(d):
        rows = pl.ds(pl.multiple_of(((z + 4 + turn * d) % 4) * 2 * tr, 2 * tr), 2 * tr)
        for yy in range(2):
            go(("p", d, yy), a.at[rows, cols(yy, 1 - k)], sb.at[d, yy], s_dev)

    def reduce1(d):
        start = pl.multiple_of(((z + 4 + turn * d) % 4) * 2 * tr, 2 * tr)
        for yy in range(2):
            got(("p", d, yy), sb.at[d, yy], s_dev)
            add(start, 2 * tr, cols(yy, k), sb.at[d, yy])
        for i in range(2):
            go(("ry1", d, i), blk(d, i, 1 - y, k, 0), ry1.at[d, i], y_dev)
            go(("rx1", d, i), blk(d, 1 - x, i, k, 1), rx1.at[d, i], x_dev)

    def reduce2(d):
        for i in range(2):
            got(("ry1", d, i), ry1.at[d, i], y_dev)
            add(row(d, i), half, cols(y, k), ry1.at[d, i])
        go(("rx2", d), blk(d, 1 - x, y, k, 0), rx2.at[d], x_dev)
        for i in range(2):
            got(("rx1", d, i), rx1.at[d, i], x_dev)
            add(row(d, x) + half, half, cols(i, k), rx1.at[d, i])
        go(("ry2", d), blk(d, x, 1 - y, k, 1), ry2.at[d], y_dev)

    def reduce3(d):
        got(("rx2", d), rx2.at[d], x_dev)
        add(row(d, x), half, cols(y, k), rx2.at[d])
        got(("ry2", d), ry2.at[d], y_dev)
        add(row(d, x) + half, half, cols(y, k), ry2.at[d])
        if d:
            go(("rz", d), blk(d, x, y, k), rz.at[seen(d) - 1], z_dev(d), SLOT["rz", 1] + seen(d) - 1)

    pass_xy(0)
    pass_z(1)
    loads[0].wait()
    pass_far(0)
    loads[1].wait()
    for m in range(1, 8):
        got(("w", m), gates.at[(dp + m) % 8], ((dp + m) % 8, ex))
    for load in loads[2:]:
        load.wait()

    for i, d in enumerate(ORDER):
        complete(d)
        hidden(d)
        if i == 0:
            pass_z(2)
        if i < 3:
            pass_xy(ORDER[i + 1])
        project(d)
        reduce0(d)
        if i == 0:
            pass_z(3)
        if i < 3:
            pass_far(ORDER[i + 1])
        if i >= 1:
            reduce1(ORDER[i - 1])
        if i >= 2:
            reduce2(ORDER[i - 2])
        if i >= 3:
            reduce3(ORDER[i - 3])
    reduce1(ORDER[3])
    reduce2(ORDER[2])
    reduce3(ORDER[1])
    reduce2(ORDER[3])
    reduce3(ORDER[2])
    reduce3(ORDER[3])
    for d in (1, 2, 3):
        got(("rz", d), rz.at[d - 1], z_dev(d))

    @pl.loop(0, tr // 64)
    def _(i):
        o = pl.multiple_of(i * 64, 64)
        total = a[pl.ds(pl.multiple_of(row(0, x) + o, 64), 64), cols(y, k)].astype(jnp.float32)
        for d in range(3):
            total = total + rz[d, pl.ds(o, 64), :].astype(jnp.float32)
        out[pl.ds(o, 64), :] = total.astype(jnp.bfloat16)

    for name in list(sent):
        drain(name)


def fused_body(tokens, route_ids, route_gates, gate_weight, up_weight, down_weight):
    tr, tc = tokens.shape
    width = gate_weight.shape[2]
    hid = gate_weight.shape[1]
    experts = lax.axis_index("expert") * EXP_DEV + jnp.arange(EXP_DEV, dtype=jnp.int32)
    hit = route_ids[None, :, :] == experts[:, None, None]
    wt = jnp.sum(jnp.where(hit, route_gates[None, :, :], 0.0), axis=2)
    half = tr // 2
    bf = jnp.bfloat16
    return pl.pallas_call(
        layer_kernel,
        out_shape=jax.ShapeDtypeStruct((tr, tc), bf),
        in_specs=[
            pl.BlockSpec(memory_space=pl.ANY),
            pl.BlockSpec(memory_space=pltpu.VMEM),
            pl.BlockSpec(memory_space=pl.ANY),
            pl.BlockSpec(memory_space=pl.ANY),
            pl.BlockSpec(memory_space=pl.ANY),
        ],
        out_specs=pl.BlockSpec(memory_space=pltpu.VMEM),
        scratch_shapes=[
            pltpu.VMEM((8 * tr, width), bf),
            pltpu.VMEM((8, EXP_DEV, tr), jnp.float32),
            pltpu.VMEM((hid, width), bf),
            pltpu.VMEM((hid, width), bf),
            pltpu.VMEM((hid, width), bf),
            pltpu.VMEM((4, 2, 2 * tr, tc), bf),
            pltpu.VMEM((4, 2, half, tc), bf),
            pltpu.VMEM((4, 2, half, tc), bf),
            pltpu.VMEM((4, half, tc), bf),
            pltpu.VMEM((4, half, tc), bf),
            pltpu.VMEM((3, tr, tc), bf),
            pltpu.VMEM((2 * tr, hid), bf),
            pltpu.VMEM((2 * tr, 128), jnp.float32),
            pltpu.SemaphoreType.DMA((len(NAMES),)),
            pltpu.SemaphoreType.DMA((len(NAMES),)),
            pltpu.SemaphoreType.DMA((5,)),
        ],
        compiler_params=pltpu.CompilerParams(
            collective_id=0, has_side_effects=True, vmem_limit_bytes=60 * 1024 * 1024
        ),
        cost_estimate=pl.CostEstimate(
            flops=6 * 8 * tr * width * hid, bytes_accessed=6 * width * hid, transcendentals=0
        ),
    )(tokens, wt, gate_weight[0], up_weight[0], down_weight[0])


def route_slots(ids_rows, first_expert, expert_count, capacity):
    tok_rows, top_k = ids_rows.shape
    flat_ids = ids_rows.reshape(-1)
    local_ids = flat_ids - first_expert
    inside = (local_ids >= 0) & (local_ids < expert_count)
    safe_ids = jnp.where(inside, local_ids, 0)
    onehot = (safe_ids[:, None] == jnp.arange(expert_count, dtype=jnp.int32)[None, :]).astype(
        jnp.int32
    )
    onehot = onehot * inside.astype(jnp.int32)[:, None]
    running = jnp.cumsum(onehot, axis=0) - 1
    position = jnp.sum(onehot * running, axis=1)
    dump_slot = expert_count * capacity
    slot_index = jnp.where(inside, safe_ids * capacity + position, dump_slot)
    owner = jnp.arange(tok_rows * top_k, dtype=jnp.int32) // top_k
    slot_token = jnp.full((dump_slot + 1,), tok_rows, jnp.int32).at[slot_index].set(owner)
    return (slot_index, slot_token[:dump_slot])


def expert_rows(rows, gate_rows, up_rows, down_rows):
    dims = (((1,), (1,)), ((), ()))
    gate = lax.dot_general(rows, gate_rows, dims, preferred_element_type=jnp.float32)
    upper = lax.dot_general(rows, up_rows, dims, preferred_element_type=jnp.float32)
    act = (jax.nn.silu(gate) * upper).astype(jnp.bfloat16)
    return jnp.dot(act, down_rows, preferred_element_type=jnp.float32)


def body(tokens, route_ids, route_gates, gate_weight, up_weight, down_weight):
    gate_local = gate_weight[0]
    up_local = up_weight[0]
    down_local = down_weight[0]
    columns = lax.axis_size("expert")
    dp_count = lax.axis_size("dp")
    blocks = dp_count // EXP_DEV
    column = lax.axis_index("expert")
    rows_all = lax.all_gather(tokens, "expert", axis=1, tiled=True)
    tok_rows, top_k = route_ids.shape
    width = rows_all.shape[1]
    capacity = 2 * tok_rows * top_k // (EXP_DEV * columns)
    slot_index, slot_token = route_slots(route_ids, column * EXP_DEV, EXP_DEV, capacity)
    padded = jnp.concatenate([rows_all, jnp.zeros((1, width), jnp.bfloat16)], axis=0)
    buffer = padded[slot_token].reshape(EXP_DEV, capacity, width)
    copies = jnp.broadcast_to(buffer[:, None], (EXP_DEV, blocks, capacity, width))
    copies = copies.reshape(dp_count, capacity, width)
    received = lax.all_to_all(copies, "dp", split_axis=0, concat_axis=0, tiled=True)
    count = received.shape[1]
    flat = received.reshape(dp_count * count, width)
    part = expert_rows(flat, gate_local, up_local, down_local)
    part = part.reshape(dp_count, count, width)
    partials = lax.all_to_all(
        part.astype(jnp.bfloat16), "dp", split_axis=0, concat_axis=0, tiled=True
    ).astype(part.dtype)
    results = jnp.sum(partials.reshape(EXP_DEV, blocks, capacity, width), axis=1).astype(
        jnp.bfloat16
    )
    results = results.reshape(EXP_DEV * capacity, width)
    results_pad = jnp.concatenate([results, jnp.zeros((1, width), jnp.bfloat16)], axis=0)
    slot_rows = slot_index.reshape(tok_rows, top_k)
    mixed = jnp.zeros((tok_rows, width), jnp.float32)
    for route in range(top_k):
        picked = results_pad[slot_rows[:, route]]
        mixed = mixed + route_gates[:, route : route + 1] * picked.astype(jnp.float32)
    summed = lax.psum_scatter(mixed, "expert", scatter_dimension=1, tiled=True)
    return summed.astype(jnp.bfloat16)


def solution(mesh):
    placed = (
        P("dp", "expert"),
        P("dp", None),
        P("dp", None),
        P("expert", "dp", None),
        P("expert", "dp", None),
        P("expert", "dp", None),
    )
    small = mesh.shape["dp"] == 8 and mesh.shape["expert"] == 4
    return jax.shard_map(
        fused_body if small else body, mesh=mesh, in_specs=placed, out_specs=P("dp", "expert"), check_vma=False
    )
```
